128 devices in a mesh: outer: 8 (over y, core), inner: 16 (over x, z).
Axes of the slice: x: 4, y: 4, z: 4, core: 2. Of those that a mesh axis runs over, the one named last changes fastest.
Arguments:
- currents: bfloat16 [16, 262144], P(None, ('outer', 'inner')), may hold values from -6 to 6
- near_blocks: bfloat16 [1024, 16, 256, 256], P(('outer', 'inner')), may hold values from -0.09375 to 0.09375
- near_cols: int32 [1024, 16], P(('outer', 'inner')), may hold values from 0 to 1023, as said below
- row_factors: bfloat16 [8, 32, 262144], P(None, None, ('outer', 'inner')), may hold values from -0.03125 to 0.03125
- col_factors: bfloat16 [8, 32, 262144], P(None, None, ('outer', 'inner')), may hold values from -0.375 to 0.375
- resistance: float32 [262144], P(('outer', 'inner')), may hold values from 0.2 to 2
Outputs:
- voltages: float32 [16, 262144], P(None, ('outer', 'inner'))
The draws below stay inside these ranges and needn't reach their ends.
Inputs may be any that keep to these rules, and one draw needn't show every extreme that they name: `near_cols`: blocks are owned by devices in order, 8 to a device (outer index major). Every near column lies in the row's own group or one of the two groups next to it in circular order. Among the 128 near blocks of one device's rows, at most 3 have their column on any one device, and exactly 3 have it on the owning device itself.
All inputs are finite; a program needn't handle non-finite values.
Results may differ from the reference program's by a relative error of at most 0.0016.
Values may be sent and summed in bfloat16 or wider, within the bound.
No kernel may reach another device: no remote copies, remote signals or barrier semaphores. Data moves between devices by JAX's collectives and lax.ppermute only.
A program may use at most 128 MiB of HBM per device.

```python
import math
import jax
import jax.numpy as jnp
from jax import lax

BLK = 256
NRHS = 16
RANK = 32
KN = 16
BPD = 8
NB = 1024
N = 262144
N_OUTER = 8
N_INNER = 16


def draw_near_cols(key, part):
    key = jax.random.fold_in(key, 11)
    devices = N_OUTER * N_INNER
    pairs = BPD * KN
    reach = 3 * N_INNER
    capacity = max(2, (pairs + reach - 1) // reach)
    keys = jax.random.split(key, devices)

    def one_device(subkey, owner):
        first, second, third = jax.random.split(subkey, 3)
        group = owner // N_INNER
        own_pos = N_INNER + owner % N_INNER
        slots = jax.random.permutation(first, (reach - 1) * capacity)[:pairs - capacity]
        candidate = slots // capacity
        position = candidate + (candidate >= own_pos).astype(jnp.int32)
        offset = position // N_INNER
        inner_pos = position % N_INNER
        others = ((group + offset - 1) % N_OUTER * N_INNER + inner_pos).astype(jnp.int32)
        target = jnp.concatenate([jnp.full((capacity,), owner, jnp.int32), others])
        target = jax.random.permutation(second, target)
        local_block = jax.random.randint(third, (pairs,), 0, BPD)
        return (target * BPD + local_block).astype(jnp.int32)
    columns = jax.vmap(one_device)(keys, jnp.arange(devices, dtype=jnp.int32))
    return columns.reshape(NB, KN)


def block_levels(stream_key, shape, cuts, least, top_value):
    loudness = 1.0
    for axis_at, shards_of in cuts:
        heights = jax.random.uniform(jax.random.fold_in(jax.random.fold_in(stream_key, 6), axis_at), (shards_of,), jnp.float32, least / len(cuts), top_value / len(cuts))
        loudness = loudness * jnp.repeat(jnp.exp(heights), shape[axis_at] // shards_of).reshape((-1,) + (1,) * (len(shape) - 1 - axis_at))
    return loudness


def centred(own_key, dims, width, limit, cuts=(), held_as=jnp.bfloat16):
    drawn = width * jax.random.normal(own_key, dims, jnp.float32)
    if cuts:
        drawn = drawn * block_levels(own_key, dims, cuts, -0.22, 0.18)
    return jnp.clip(drawn, -limit, limit).astype(held_as)


def setup_inputs(seed: int = 0) -> dict:
    streams_of = jax.random.split(jax.random.key(seed), 7)
    return {
        "currents": centred(streams_of[0], (NRHS, N), 1.0, 6.0, ((1, 128),)),
        "near_blocks": centred(streams_of[1], (NB, KN, BLK, BLK), (KN * BLK) ** -0.5, 0.09375, ((0, 128),)),
        "near_cols": draw_near_cols(jax.random.fold_in(streams_of[6], 71), 0),
        "row_factors": centred(streams_of[3], (N_OUTER, RANK, N), (N // N_OUTER) ** -0.5, 0.03125, ((2, 128),)),
        "col_factors": centred(streams_of[4], (N_OUTER, RANK, N), (RANK * N_OUTER) ** -0.5, 0.375, ((2, 128),)),
        "resistance": jnp.clip(jnp.exp(math.log(2.0) - 2.3025851 * jax.random.uniform(streams_of[5], (N,), jnp.float32) ** block_levels(streams_of[5], (N,), ((0, 128),), -0.2, 0.2)), 0.2, 2.0),
    }


def reference(currents, near_blocks, near_cols, row_factors, col_factors, resistance):
    stride = math.gcd(NB, 16)
    by_block = currents.reshape(NRHS, NB, BLK).transpose(1, 0, 2)

    def advance(accumulator, block_step):
        start = (block_step * stride).astype(jnp.int32)
        current_piece = lax.dynamic_slice_in_dim(by_block, start, stride, 0).astype(jnp.float32)
        block_piece = lax.dynamic_slice_in_dim(near_blocks, start, stride, 0).astype(jnp.float32)
        column_piece = lax.dynamic_slice_in_dim(near_cols, start, stride, 0)
        products = jnp.einsum('bsp,bkpq->bksq', current_piece, block_piece, precision=lax.Precision.HIGHEST)
        accumulator = accumulator.at[column_piece.reshape(-1)].add(products.reshape(-1, NRHS, BLK))
        return accumulator, None

    start_acc = jnp.zeros((NB, NRHS, BLK), jnp.float32)
    accumulator, _ = lax.scan(advance, start_acc, jnp.arange(NB // stride, dtype=jnp.int32))
    near = accumulator.transpose(1, 0, 2).reshape(NRHS, N)
    groups = jnp.arange(N_OUTER, dtype=jnp.int32)
    ahead = (groups[None, :] - groups[:, None]) % N_OUTER
    distance = jnp.minimum(ahead, N_OUTER - ahead)
    far_mask = (distance >= 1).astype(jnp.float32)
    group_len = N // N_OUTER
    grouped = currents.astype(jnp.float32).reshape(NRHS, N_OUTER, group_len)
    left = row_factors.astype(jnp.float32).reshape(N_OUTER, RANK, N_OUTER, group_len)
    coef = jnp.einsum('hrgn,sgn->ghrs', left, grouped, precision=lax.Precision.HIGHEST).astype(jnp.bfloat16)
    masked = coef.astype(jnp.float32) * far_mask[:, :, None, None]
    right = col_factors.astype(jnp.float32).reshape(N_OUTER, RANK, N_OUTER, group_len)
    far = jnp.einsum('grhn,ghrs->shn', right, masked, precision=lax.Precision.HIGHEST).reshape(NRHS, N)
    return near + far + resistance[None, :] * currents.astype(jnp.float32)
```

```python
import jax
import jax.numpy as jnp
from jax import lax
from jax.experimental import pallas as pl
from jax.experimental.pallas import tpu as pltpu
from jax.sharding import PartitionSpec as P

SIDES = 16
BLK = 256
KN = 16
BPD = 8
GROUPS = 8
INNER = 16
RANK = 32
CAP = 3
SLOTS = 3 * CAP
NEAR_ROWS = SLOTS * SIDES
ROWS = NEAR_ROWS + 2 * SIDES
NOWHERE = 64.0
STEP_BLOCKS = 8
F32 = jnp.float32
BF16 = jnp.bfloat16


def lanes(shape):
    return lax.broadcasted_iota(jnp.int32, shape, len(shape) - 1)


def term_kernel(cur_ref, row_ref, out_ref):
    term = lax.dot_general(
        cur_ref[...], row_ref[...], (((1,), (1,)), ((), ())), preferred_element_type=F32
    )
    for h in range(GROUPS):
        out_ref[h] = term[:, h * RANK : (h + 1) * RANK]


def near_kernel(cols_ref, me_ref, cur_ref, blocks_ref, out_ref, meta_ref, count_ref):
    step = pl.program_id(0)
    group = me_ref[0]

    @pl.when(step == 0)
    def _():
        for t in range(3 * INNER):
            count_ref[t] = 0
        meta_ref[...] = jnp.full_like(meta_ref, NOWHERE)
        out_ref[...] = jnp.zeros_like(out_ref)

    currents = cur_ref[...]
    place = lanes((SIDES, BLK))
    for j in range(STEP_BLOCKS):
        product = jnp.dot(currents, blocks_ref[j], preferred_element_type=F32)
        col = cols_ref[step * STEP_BLOCKS + j]
        target_group = col >> 7
        target = (col >> 3) & (INNER - 1)
        apart = target_group ^ group
        kind = jnp.where(apart == 0, 0, jnp.where(apart == 1, 1, 2))
        used = count_ref[kind * INNER + target]
        count_ref[kind * INNER + target] = used + 1
        slot = kind * CAP + used
        row = pl.multiple_of(slot * SIDES, SIDES)
        out_ref[target, pl.ds(row, SIDES), :] = product.astype(BF16)
        here = place == group * RANK + slot
        meta_ref[target] = jnp.where(here, (col & (BPD - 1)).astype(F32), meta_ref[target])

    @pl.when(step == pl.num_programs(0) - 1)
    def _():
        out_ref[:, NEAR_ROWS + SIDES :, :] = meta_ref[...].astype(BF16)


def far_rows_kernel(me_ref, held_ref, arrived_ref, out_ref):
    low_half = pl.program_id(0) == 1
    whole = jnp.concatenate([arrived_ref[g] for g in range(GROUPS)], axis=1)
    high = whole.astype(BF16)

    @pl.when(jnp.logical_not(low_half))
    def _():
        out_ref[...] = jnp.broadcast_to(high[None], out_ref.shape)

    @pl.when(low_half)
    def _():
        low = whole - high.astype(F32)
        own = lanes((INNER, SIDES, BLK)) // RANK == me_ref[0]
        out_ref[...] = jnp.where(own, held_ref[...].astype(F32), low[None]).astype(BF16)


def gather_kernel(me_ref, got_ref, own_ref, core_ref, next_ref):
    lows = got_ref[:, NEAR_ROWS + SIDES :, :].reshape(INNER * SIDES, BLK)
    from_lane = lax.broadcasted_iota(jnp.int32, (BLK, BLK), 0)
    to_lane = lanes((BLK, BLK))
    spread = jnp.where(from_lane == me_ref[0] * RANK + to_lane // SIDES, float(SIDES), 0.0)
    places = jnp.dot(lows, spread.astype(BF16), preferred_element_type=F32)
    lane = lanes((SIDES, BLK))
    shift = (lane % SIDES + lane // (CAP * SIDES) * (BPD * SIDES)).astype(F32)
    rows = lax.broadcasted_iota(jnp.int32, (3 * BPD * SIDES, NEAR_ROWS), 0).astype(F32)
    total = jnp.zeros((3 * BPD * SIDES, BLK), F32)
    for i in range(INNER):
        place = (places[i * SIDES : (i + 1) * SIDES] + shift)[:, :NEAR_ROWS]
        pick = jnp.where(jnp.tile(place, (3 * BPD, 1)) == rows, 1.0, 0.0).astype(BF16)
        total += jnp.dot(pick, got_ref[i, :NEAR_ROWS, :], preferred_element_type=F32)
    size = BPD * SIDES
    own_ref[...] = total[:size]
    core_ref[...] = total[size : 2 * size]
    next_ref[...] = total[2 * size :]


def far_kernel(me_ref, got_ref, col_ref, res_ref, cur_ref, near_ref, out_ref):
    total = jnp.zeros((SIDES, BLK), F32)
    for i in range(INNER):
        high = got_ref[i, :SIDES, :].astype(F32)
        low = got_ref[i, SIDES:, :].astype(F32)
        total += high + low
    coef = jnp.where(lanes((SIDES, BLK)) // RANK == me_ref[0], 0.0, total).astype(BF16)
    far = jnp.dot(coef, col_ref[...], preferred_element_type=F32)
    far += res_ref[...] * cur_ref[...].astype(F32)
    for b in range(BPD):
        cut = slice(b * BLK, (b + 1) * BLK)
        out_ref[:, cut] = far[:, cut] + near_ref[b * SIDES : (b + 1) * SIDES, :]


def add_kernel(base_ref, core_ref, next_ref, out_ref):
    for b in range(BPD):
        cut = slice(b * BLK, (b + 1) * BLK)
        rows = slice(b * SIDES, (b + 1) * SIDES)
        out_ref[:, cut] = base_ref[:, cut] + core_ref[rows, :] + next_ref[rows, :]


def spec(*shape):
    return pl.BlockSpec(shape, lambda *_: (0,) * len(shape))


def params():
    return pltpu.CompilerParams(vmem_limit_bytes=40 * 1024 * 1024)


def cost(flops, moved):
    return pl.CostEstimate(flops=flops, bytes_accessed=moved, transcendentals=0)


def on_device(currents, near_blocks, near_cols, row_factors, col_factors, resistance):
    filaments = currents.shape[1]
    flat = GROUPS * RANK
    group = lax.axis_index("outer")
    me = jnp.stack([group, lax.axis_index("inner")]).astype(jnp.int32)
    in_smem = pl.BlockSpec(memory_space=pltpu.SMEM)

    term = pl.pallas_call(
        term_kernel,
        out_shape=jax.ShapeDtypeStruct((GROUPS, SIDES, RANK), F32),
        compiler_params=params(),
        cost_estimate=cost(2 * SIDES * flat * filaments, 1200000),
    )(currents, row_factors.reshape(flat, filaments))
    arrived = lax.all_to_all(term, "outer", split_axis=0, concat_axis=0, tiled=True)

    blocks = BPD * KN
    steps = blocks // STEP_BLOCKS
    payload_shape = jax.ShapeDtypeStruct((INNER, ROWS, BLK), BF16)
    payload = pl.pallas_call(
        near_kernel,
        out_shape=payload_shape,
        grid_spec=pltpu.PrefetchScalarGridSpec(
            num_scalar_prefetch=2,
            grid=(steps,),
            in_specs=[
                pl.BlockSpec((SIDES, BLK), lambda i, *_: (0, i * STEP_BLOCKS // KN)),
                pl.BlockSpec((STEP_BLOCKS, BLK, BLK), lambda i, *_: (i, 0, 0)),
            ],
            out_specs=spec(INNER, ROWS, BLK),
            scratch_shapes=[
                pltpu.VMEM((INNER, SIDES, BLK), F32),
                pltpu.SMEM((3 * INNER,), jnp.int32),
            ],
        ),
        compiler_params=params(),
        cost_estimate=cost(2 * blocks * SIDES * BLK * BLK, 18000000),
    )(near_cols.reshape(-1), me, currents, near_blocks.reshape(blocks, BLK, BLK))

    half = pl.BlockSpec((INNER, SIDES, BLK), lambda i, *_: (0, SLOTS + i, 0))
    payload = pl.pallas_call(
        far_rows_kernel,
        out_shape=payload_shape,
        grid=(2,),
        in_specs=[in_smem, half, spec(GROUPS, SIDES, RANK)],
        out_specs=half,
        input_output_aliases={1: 0},
        compiler_params=params(),
        cost_estimate=cost(100000, 600000),
    )(me, payload, arrived)

    got = lax.all_to_all(payload, "inner", split_axis=0, concat_axis=0, tiled=True)

    sums = jax.ShapeDtypeStruct((BPD * SIDES, BLK), F32)
    own, to_core, to_next = pl.pallas_call(
        gather_kernel,
        out_shape=(sums, sums, sums),
        in_specs=[in_smem, pl.BlockSpec(memory_space=pltpu.VMEM)],
        compiler_params=params(),
        cost_estimate=cost(2 * 384 * 144 * 16 * 256, 2000000),
    )(me, got)
    core_pairs = [(g, g ^ 1) for g in range(GROUPS)]
    next_pairs = [(g, (g + (1 if g % 2 else -1)) % GROUPS) for g in range(GROUPS)]
    from_next = lax.ppermute(to_next, "outer", next_pairs)
    from_core = lax.ppermute(to_core, "outer", core_pairs)

    base = pl.pallas_call(
        far_kernel,
        out_shape=jax.ShapeDtypeStruct((SIDES, filaments), F32),
        grid=(1,),
        in_specs=[
            in_smem,
            pl.BlockSpec((INNER, 2 * SIDES, BLK), lambda *_: (0, 0, 0)),
            spec(flat, filaments),
            spec(1, filaments),
            spec(SIDES, filaments),
            spec(BPD * SIDES, BLK),
        ],
        out_specs=spec(SIDES, filaments),
        compiler_params=params(),
        cost_estimate=cost(2 * SIDES * flat * filaments, 1600000),
    )(
        me,
        got[:, NEAR_ROWS:, :],
        col_factors.reshape(flat, filaments),
        resistance[None, :],
        currents,
        own,
    )
    return pl.pallas_call(
        add_kernel,
        out_shape=jax.ShapeDtypeStruct((SIDES, filaments), F32),
        compiler_params=params(),
        cost_estimate=cost(100000, 600000),
    )(base, from_core, from_next)


def solution(mesh):
    return jax.shard_map(
        on_device,
        mesh=mesh,
        in_specs=(
            P(None, ("outer", "inner")),
            P(("outer", "inner"), None, None, None),
            P(("outer", "inner"), None),
            P(None, None, ("outer", "inner")),
            P(None, None, ("outer", "inner")),
            P(("outer", "inner")),
        ),
        out_specs=P(None, ("outer", "inner")),
        check_vma=False,
    )
```

```python
import jax
import jax.numpy as jnp
from jax import lax
from jax.experimental import pallas as pl
from jax.experimental.pallas import tpu as pltpu
from jax.sharding import PartitionSpec as P

SIDES = 16
BLK = 256
KN = 16
BPD = 8
BLOCKS = BPD * KN
GROUPS = 8
INNER = 16
RANK = 32
LANES = 128
CAP = 3
KIND_ROWS = CAP * SIDES
NEAR_ROWS = 3 * KIND_ROWS
ROWS = NEAR_ROWS + 2 * SIDES
SUMS = BPD * SIDES
NOWHERE = 64
PIECE = 16
F32 = jnp.float32
BF16 = jnp.bfloat16
I32 = jnp.int32


def rows_of(shape):
    return lax.broadcasted_iota(I32, shape, 0)


def lanes_of(shape):
    return lax.broadcasted_iota(I32, shape, len(shape) - 1)


def slot_of(cols, rank, group):
    apart = (cols >> 7) ^ group
    kind = jnp.where(apart == 0, 0, jnp.where(apart == 1, 1, 2))
    return kind * CAP + rank


def send_kernel(
    cols_hbm, cur_hbm, row_hbm, blocks_hbm, out_ref,
    cols_ref, cur_ref, row_ref, blocks_ref, place_ref, dest_ref, small_sem, block_sem,
):
    cols_copy = pltpu.make_async_copy(cols_hbm, cols_ref, small_sem.at[0])
    cur_copy = pltpu.make_async_copy(cur_hbm, cur_ref, small_sem.at[1])
    row_copy = pltpu.make_async_copy(row_hbm, row_ref, small_sem.at[2])
    dest_copy = pltpu.make_async_copy(place_ref, dest_ref, small_sem.at[3])
    cols_copy.start()
    cur_copy.start()
    row_copy.start()
    block_copies = []
    for c in range(BLOCKS // PIECE):
        part = pl.ds(c * PIECE, PIECE)
        copy = pltpu.make_async_copy(blocks_hbm.at[part], blocks_ref.at[part], block_sem.at[c])
        copy.start(priority=1)
        block_copies.append(copy)
    group = lax.axis_index("outer")
    for t in range(INNER):
        out_ref[t * ROWS : t * ROWS + NEAR_ROWS, :] = jnp.zeros((NEAR_ROWS, BLK), BF16)

    cols_copy.wait()
    table = cols_ref[...].astype(F32)
    spread = jnp.concatenate(
        [jnp.broadcast_to(table[b : b + 1, :], (KN, KN)) for b in range(BPD)], axis=0
    )
    shape = (BLOCKS, KN)
    picked = jnp.where(lanes_of(shape) == rows_of(shape) % KN, spread, 0.0)
    down = jnp.sum(picked, axis=1, keepdims=True)
    square = (BLOCKS, BLOCKS)
    wide = jnp.broadcast_to(down, square)
    across = wide.T[:1, :].astype(I32)
    down = down.astype(I32)
    same = (wide.astype(I32) >> 3) == (wide.T.astype(I32) >> 3)
    above = rows_of(square) < lanes_of(square)
    below = rows_of(square) > lanes_of(square)
    rank_across = jnp.sum(jnp.where(same & above, 1.0, 0.0), axis=0, keepdims=True).astype(I32)
    rank_down = jnp.sum(jnp.where(same & below, 1.0, 0.0), axis=1, keepdims=True).astype(I32)
    target = (across >> 3) & (INNER - 1)
    first_row = target * ROWS + slot_of(across, rank_across, group) * SIDES
    place_ref[...] = jnp.broadcast_to(first_row, place_ref.shape)
    dest_copy.start()
    to_target = jnp.where(rows_of((INNER, BLOCKS)) == target, 1.0, 0.0).astype(BF16)
    lane = group * RANK + slot_of(down, rank_down, group)
    block_id = ((down & (BPD - 1)) - NOWHERE).astype(F32)
    at_slot = jnp.where(lanes_of((BLOCKS, BLK)) == lane, block_id, 0.0).astype(BF16)
    ids = jnp.dot(to_target, at_slot, preferred_element_type=F32) + float(NOWHERE)

    cur_copy.wait()
    row_copy.wait()
    term = lax.dot_general(
        cur_ref[...], row_ref[...], (((1,), (1,)), ((), ())), preferred_element_type=F32
    )
    high = term.astype(BF16)
    low = term - high.astype(F32)
    own = lanes_of((SIDES, BLK)) // RANK == group
    for t in range(INNER):
        far_row = t * ROWS + NEAR_ROWS
        out_ref[far_row : far_row + SIDES, :] = high
        out_ref[far_row + SIDES : far_row + 2 * SIDES, :] = jnp.where(
            own, ids[t : t + 1, :], low
        ).astype(BF16)

    dest_copy.wait()
    for c in range(BLOCKS // PIECE):
        block_copies[c].wait()
        for e in range(c * PIECE, (c + 1) * PIECE):
            b = e // KN
            currents = cur_ref[:, b * BLK : (b + 1) * BLK]
            product = jnp.dot(currents, blocks_ref[e], preferred_element_type=F32)
            row = pl.multiple_of(dest_ref[0, e], SIDES)
            out_ref[pl.ds(row, SIDES), :] = product.astype(BF16)


def places_of(got_ref):
    group = lax.axis_index("outer")
    lows = got_ref[:, NEAR_ROWS + SIDES :, :].reshape(INNER * SIDES, BLK)
    square = (BLK, BLK)
    expand = rows_of(square) == group * RANK + lanes_of(square) // SIDES
    expand = jnp.where(expand, float(SIDES), 0.0).astype(BF16)
    places = jnp.dot(lows, expand, preferred_element_type=F32)
    lane = lanes_of((INNER * SIDES, BLK))
    return places + (lane % SIDES + lane // KIND_ROWS * SUMS).astype(F32)


def add_slots(got_ref, places, first_kind, kinds):
    start = first_kind * KIND_ROWS
    stop = start + kinds * KIND_ROWS
    rows = (rows_of((kinds * SUMS, stop - start)) + first_kind * SUMS).astype(F32)
    total = jnp.zeros((kinds * SUMS, BLK), F32)
    for i in range(INNER):
        place = places[i * SIDES : (i + 1) * SIDES, start:stop]
        pick = jnp.where(jnp.tile(place, (kinds * BPD, 1)) == rows, 1.0, 0.0).astype(BF16)
        total += jnp.dot(pick, got_ref[i, start:stop, :], preferred_element_type=F32)
    return total


def sum_kernel(got_ref, core_ref, next_ref, coef_ref):
    total = add_slots(got_ref, places_of(got_ref), 1, 2)
    core_ref[...] = total[:SUMS]
    next_ref[...] = total[SUMS:]
    coef = jnp.zeros((SIDES, BLK), F32)
    for i in range(INNER):
        high = got_ref[i, NEAR_ROWS : NEAR_ROWS + SIDES, :].astype(F32)
        low = got_ref[i, NEAR_ROWS + SIDES :, :].astype(F32)
        coef += high + low
    coef_ref[...] = jnp.zeros_like(coef_ref)
    for h in range(GROUPS):
        coef_ref[h, :, :RANK] = coef[:, h * RANK : (h + 1) * RANK].astype(BF16)


def own_kernel(got_ref, res_ref, cur_ref, out_ref):
    total = add_slots(got_ref, places_of(got_ref), 0, 1)
    for b in range(BPD):
        cut = slice(b * BLK, (b + 1) * BLK)
        diagonal = res_ref[:, cut] * cur_ref[:, cut].astype(F32)
        out_ref[:, cut] = diagonal + total[b * SIDES : (b + 1) * SIDES, :]


def final_kernel(coef_ref, col_ref, base_ref, core_ref, next_ref, out_ref):
    coef = jnp.concatenate([coef_ref[g, :, :RANK] for g in range(GROUPS)], axis=1)
    own = lanes_of((SIDES, BLK)) // RANK == lax.axis_index("outer")
    coef = jnp.where(own, 0.0, coef.astype(F32)).astype(BF16)
    far = jnp.dot(coef, col_ref[...], preferred_element_type=F32)
    for b in range(BPD):
        cut = slice(b * BLK, (b + 1) * BLK)
        rows = slice(b * SIDES, (b + 1) * SIDES)
        near = base_ref[:, cut] + core_ref[rows, :] + next_ref[rows, :]
        out_ref[:, cut] = far[:, cut] + near


def params(mebibytes=12):
    return pltpu.CompilerParams(vmem_limit_bytes=mebibytes * 1024 * 1024)


def cost(flops, moved):
    return pl.CostEstimate(flops=flops, bytes_accessed=moved, transcendentals=0)


def on_device(currents, near_blocks, near_cols, row_factors, col_factors, resistance):
    filaments = currents.shape[1]
    flat = GROUPS * RANK
    in_vmem = pl.BlockSpec(memory_space=pltpu.VMEM)
    anywhere = pl.BlockSpec(memory_space=pl.ANY)

    payload = pl.pallas_call(
        send_kernel,
        out_shape=jax.ShapeDtypeStruct((INNER * ROWS, BLK), BF16),
        in_specs=[anywhere] * 4,
        out_specs=in_vmem,
        scratch_shapes=[
            pltpu.VMEM((BPD, KN), I32),
            pltpu.VMEM((SIDES, filaments), BF16),
            pltpu.VMEM((flat, filaments), BF16),
            pltpu.VMEM((BLOCKS, BLK, BLK), BF16),
            pltpu.VMEM((8, BLOCKS), I32),
            pltpu.SMEM((8, BLOCKS), I32),
            pltpu.SemaphoreType.DMA((4,)),
            pltpu.SemaphoreType.DMA((BLOCKS // PIECE,)),
        ],
        compiler_params=params(56),
        cost_estimate=cost(2 * BLOCKS * SIDES * BLK * BLK, 18000000),
    )(
        near_cols,
        currents,
        row_factors.reshape(flat, filaments),
        near_blocks.reshape(BLOCKS, BLK, BLK),
    )

    got = lax.all_to_all(
        payload.reshape(INNER, ROWS, BLK), "inner", split_axis=0, concat_axis=0, tiled=True
    )

    sums = jax.ShapeDtypeStruct((SUMS, BLK), F32)
    to_core, to_next, coef = pl.pallas_call(
        sum_kernel,
        out_shape=(sums, sums, jax.ShapeDtypeStruct((GROUPS, SIDES, LANES), BF16)),
        compiler_params=params(),
        cost_estimate=cost(2 * 256 * 96 * 16 * 256, 2000000),
    )(got)
    core_pairs = [(g, g ^ 1) for g in range(GROUPS)]
    next_pairs = [(g, (g + (1 if g % 2 else -1)) % GROUPS) for g in range(GROUPS)]
    from_next = lax.ppermute(to_next, "outer", next_pairs)
    from_core = lax.ppermute(to_core, "outer", core_pairs)
    coef = lax.all_to_all(coef, "outer", split_axis=0, concat_axis=0, tiled=True)

    base = pl.pallas_call(
        own_kernel,
        out_shape=jax.ShapeDtypeStruct((SIDES, filaments), F32),
        compiler_params=params(),
        cost_estimate=cost(2 * 128 * 48 * 16 * 256, 2000000),
    )(got, resistance[None, :], currents)
    return pl.pallas_call(
        final_kernel,
        out_shape=jax.ShapeDtypeStruct((SIDES, filaments), F32),
        compiler_params=params(),
        cost_estimate=cost(2 * SIDES * flat * filaments, 1600000),
    )(coef, col_factors.reshape(flat, filaments), base, from_core, from_next)


def solution(mesh):
    return jax.shard_map(
        on_device,
        mesh=mesh,
        in_specs=(
            P(None, ("outer", "inner")),
            P(("outer", "inner"), None, None, None),
            P(("outer", "inner"), None),
            P(None, None, ("outer", "inner")),
            P(None, None, ("outer", "inner")),
            P(("outer", "inner")),
        ),
        out_specs=P(None, ("outer", "inner")),
        check_vma=False,
    )
```

```python
import jax
import jax.numpy as jnp
from jax import lax
from jax.experimental import pallas as pl
from jax.experimental.pallas import tpu as pltpu
from jax.sharding import PartitionSpec as P

SIDES = 16
BLK = 256
KN = 16
BPD = 8
BLOCKS = BPD * KN
GROUPS = 8
INNER = 16
RANK = 32
LANES = 128
CAP = 3
KIND_ROWS = CAP * SIDES
NEAR_ROWS = 3 * KIND_ROWS
ROWS = NEAR_ROWS + 2 * SIDES
SUMS = BPD * SIDES
NOWHERE = 64
PIECE = 16
F32 = jnp.float32
BF16 = jnp.bfloat16
I32 = jnp.int32


def rows_of(shape):
    return lax.broadcasted_iota(I32, shape, 0)


def lanes_of(shape):
    return lax.broadcasted_iota(I32, shape, len(shape) - 1)


def slot_of(cols, rank, group):
    apart = (cols >> 7) ^ group
    kind = jnp.where(apart == 0, 0, jnp.where(apart == 1, 1, 2))
    return kind * CAP + rank


def send_kernel(
    cols_hbm, cur_hbm, row_hbm, blocks_hbm, out_ref,
    cols_ref, cur_ref, row_ref, blocks_ref, place_ref, dest_ref, small_sem, block_sem,
):
    cols_copy = pltpu.make_async_copy(cols_hbm, cols_ref, small_sem.at[0])
    cur_copy = pltpu.make_async_copy(cur_hbm, cur_ref, small_sem.at[1])
    row_copy = pltpu.make_async_copy(row_hbm, row_ref, small_sem.at[2])
    dest_copy = pltpu.make_async_copy(place_ref, dest_ref, small_sem.at[3])
    cols_copy.start()
    cur_copy.start()
    row_copy.start()
    block_copies = []
    for c in range(BLOCKS // PIECE):
        part = pl.ds(c * PIECE, PIECE)
        copy = pltpu.make_async_copy(blocks_hbm.at[part], blocks_ref.at[part], block_sem.at[c])
        copy.start(priority=1)
        block_copies.append(copy)
    group = lax.axis_index("outer")
    for t in range(INNER):
        out_ref[t * ROWS : t * ROWS + NEAR_ROWS, :] = jnp.zeros((NEAR_ROWS, BLK), BF16)

    cols_copy.wait()
    table = cols_ref[...].astype(F32)
    spread = jnp.concatenate(
        [jnp.broadcast_to(table[b : b + 1, :], (KN, KN)) for b in range(BPD)], axis=0
    )
    shape = (BLOCKS, KN)
    picked = jnp.where(lanes_of(shape) == rows_of(shape) % KN, spread, 0.0)
    down = jnp.sum(picked, axis=1, keepdims=True)
    square = (BLOCKS, BLOCKS)
    wide = jnp.broadcast_to(down, square)
    across = wide.T[:1, :].astype(I32)
    down = down.astype(I32)
    same = (wide.astype(I32) >> 3) == (wide.T.astype(I32) >> 3)
    above = rows_of(square) < lanes_of(square)
    below = rows_of(square) > lanes_of(square)
    rank_across = jnp.sum(jnp.where(same & above, 1.0, 0.0), axis=0, keepdims=True).astype(I32)
    rank_down = jnp.sum(jnp.where(same & below, 1.0, 0.0), axis=1, keepdims=True).astype(I32)
    target = (across >> 3) & (INNER - 1)
    first_row = target * ROWS + slot_of(across, rank_across, group) * SIDES
    place_ref[...] = jnp.broadcast_to(first_row, place_ref.shape)
    dest_copy.start()
    to_target = jnp.where(rows_of((INNER, BLOCKS)) == target, 1.0, 0.0).astype(BF16)
    lane = group * RANK + slot_of(down, rank_down, group)
    block_id = ((down & (BPD - 1)) - NOWHERE).astype(F32)
    at_slot = jnp.where(lanes_of((BLOCKS, BLK)) == lane, block_id, 0.0).astype(BF16)
    ids = jnp.dot(to_target, at_slot, preferred_element_type=F32) + float(NOWHERE)

    cur_copy.wait()
    row_copy.wait()
    term = lax.dot_general(
        cur_ref[...], row_ref[...], (((1,), (1,)), ((), ())), preferred_element_type=F32
    )
    high = term.astype(BF16)
    low = term - high.astype(F32)
    own = lanes_of((SIDES, BLK)) // RANK == group
    for t in range(INNER):
        far_row = t * ROWS + NEAR_ROWS
        out_ref[far_row : far_row + SIDES, :] = high
        out_ref[far_row + SIDES : far_row + 2 * SIDES, :] = jnp.where(
            own, ids[t : t + 1, :], low
        ).astype(BF16)

    dest_copy.wait()
    for c in range(BLOCKS // PIECE):
        block_copies[c].wait()
        for e in range(c * PIECE, (c + 1) * PIECE):
            b = e // KN
            currents = cur_ref[:, b * BLK : (b + 1) * BLK]
            product = jnp.dot(currents, blocks_ref[e], preferred_element_type=F32)
            row = pl.multiple_of(dest_ref[0, e], SIDES)
            out_ref[pl.ds(row, SIDES), :] = product.astype(BF16)


def places_of(got_ref):
    group = lax.axis_index("outer")
    lows = got_ref[:, NEAR_ROWS + SIDES :, :].reshape(INNER * SIDES, BLK)
    square = (BLK, BLK)
    expand = rows_of(square) == group * RANK + lanes_of(square) // SIDES
    expand = jnp.where(expand, float(SIDES), 0.0).astype(BF16)
    places = jnp.dot(lows, expand, preferred_element_type=F32)
    lane = lanes_of((INNER * SIDES, BLK))
    return places + (lane % SIDES + lane // KIND_ROWS * SUMS).astype(F32)


def add_slots(got_ref, places, first_kind, kinds):
    start = first_kind * KIND_ROWS
    stop = start + kinds * KIND_ROWS
    rows = (rows_of((kinds * SUMS, stop - start)) + first_kind * SUMS).astype(F32)
    total = jnp.zeros((kinds * SUMS, BLK), F32)
    for i in range(INNER):
        place = places[i * SIDES : (i + 1) * SIDES, start:stop]
        pick = jnp.where(jnp.tile(place, (kinds * BPD, 1)) == rows, 1.0, 0.0).astype(BF16)
        total += jnp.dot(pick, got_ref[i, start:stop, :], preferred_element_type=F32)
    return total


def coef_kernel(got_ref, coef_ref):
    coef = jnp.zeros((SIDES, BLK), F32)
    for i in range(INNER):
        high = got_ref[i, :SIDES, :].astype(F32)
        low = got_ref[i, SIDES:, :].astype(F32)
        coef += high + low
    coef_ref[...] = jnp.zeros_like(coef_ref)
    for h in range(GROUPS):
        coef_ref[h, :, :RANK] = coef[:, h * RANK : (h + 1) * RANK].astype(BF16)


def sum_kernel(got_ref, res_ref, cur_ref, after_ref, core_ref, next_ref, out_ref):
    del after_ref
    places = places_of(got_ref)
    total = add_slots(got_ref, places, 1, 2)
    core_ref[...] = total[:SUMS]
    next_ref[...] = total[SUMS:]
    total = add_slots(got_ref, places, 0, 1)
    for b in range(BPD):
        cut = slice(b * BLK, (b + 1) * BLK)
        diagonal = res_ref[:, cut] * cur_ref[:, cut].astype(F32)
        out_ref[:, cut] = diagonal + total[b * SIDES : (b + 1) * SIDES, :]


def final_kernel(coef_ref, col_ref, base_ref, core_ref, next_ref, out_ref):
    coef = jnp.concatenate([coef_ref[g, :, :RANK] for g in range(GROUPS)], axis=1)
    own = lanes_of((SIDES, BLK)) // RANK == lax.axis_index("outer")
    coef = jnp.where(own, 0.0, coef.astype(F32)).astype(BF16)
    far = jnp.dot(coef, col_ref[...], preferred_element_type=F32)
    for b in range(BPD):
        cut = slice(b * BLK, (b + 1) * BLK)
        rows = slice(b * SIDES, (b + 1) * SIDES)
        near = base_ref[:, cut] + core_ref[rows, :] + next_ref[rows, :]
        out_ref[:, cut] = far[:, cut] + near


def params(mebibytes=12):
    return pltpu.CompilerParams(vmem_limit_bytes=mebibytes * 1024 * 1024)


def cost(flops, moved):
    return pl.CostEstimate(flops=flops, bytes_accessed=moved, transcendentals=0)


def in_hbm(array):
    return pltpu.with_memory_space_constraint(array, pltpu.HBM)


def on_device(currents, near_blocks, near_cols, row_factors, col_factors, resistance):
    filaments = currents.shape[1]
    flat = GROUPS * RANK
    in_vmem = pl.BlockSpec(memory_space=pltpu.VMEM)
    anywhere = pl.BlockSpec(memory_space=pl.ANY)

    payload = pl.pallas_call(
        send_kernel,
        out_shape=jax.ShapeDtypeStruct((INNER * ROWS, BLK), BF16),
        in_specs=[anywhere] * 4,
        out_specs=in_vmem,
        scratch_shapes=[
            pltpu.VMEM((BPD, KN), I32),
            pltpu.VMEM((SIDES, filaments), BF16),
            pltpu.VMEM((flat, filaments), BF16),
            pltpu.VMEM((BLOCKS, BLK, BLK), BF16),
            pltpu.VMEM((8, BLOCKS), I32),
            pltpu.SMEM((8, BLOCKS), I32),
            pltpu.SemaphoreType.DMA((4,)),
            pltpu.SemaphoreType.DMA((BLOCKS // PIECE,)),
        ],
        compiler_params=params(50),
        cost_estimate=cost(2 * BLOCKS * SIDES * BLK * BLK, 18000000),
    )(
        in_hbm(near_cols),
        in_hbm(currents),
        in_hbm(row_factors.reshape(flat, filaments)),
        in_hbm(near_blocks.reshape(BLOCKS, BLK, BLK)),
    )

    got = lax.all_to_all(
        payload.reshape(INNER, ROWS, BLK), "inner", split_axis=0, concat_axis=0, tiled=True
    )

    coef = pl.pallas_call(
        coef_kernel,
        out_shape=jax.ShapeDtypeStruct((GROUPS, SIDES, LANES), BF16),
        compiler_params=params(),
        cost_estimate=cost(200000, 300000),
    )(got[:, NEAR_ROWS:, :])
    sums = jax.ShapeDtypeStruct((SUMS, BLK), F32)
    to_core, to_next, base = pl.pallas_call(
        sum_kernel,
        out_shape=(sums, sums, jax.ShapeDtypeStruct((SIDES, filaments), F32)),
        in_specs=[in_vmem] * 3 + [anywhere],
        compiler_params=params(),
        cost_estimate=cost(2 * 384 * 96 * 16 * 256, 2000000),
    )(got, resistance[None, :], currents, coef)
    core_pairs = [(g, g ^ 1) for g in range(GROUPS)]
    next_pairs = [(g, (g + (1 if g % 2 else -1)) % GROUPS) for g in range(GROUPS)]
    from_next = lax.ppermute(to_next, "outer", next_pairs)
    from_core = lax.ppermute(to_core, "outer", core_pairs)
    coef = lax.all_to_all(coef, "outer", split_axis=0, concat_axis=0, tiled=True)

    return pl.pallas_call(
        final_kernel,
        out_shape=jax.ShapeDtypeStruct((SIDES, filaments), F32),
        compiler_params=params(),
        cost_estimate=cost(2 * SIDES * flat * filaments, 1600000),
    )(coef, col_factors.reshape(flat, filaments), base, from_core, from_next)


def solution(mesh):
    return jax.shard_map(
        on_device,
        mesh=mesh,
        in_specs=(
            P(None, ("outer", "inner")),
            P(("outer", "inner"), None, None, None),
            P(("outer", "inner"), None),
            P(None, None, ("outer", "inner")),
            P(None, None, ("outer", "inner")),
            P(("outer", "inner")),
        ),
        out_specs=P(None, ("outer", "inner")),
        check_vma=False,
    )
```

```python
import jax
import jax.numpy as jnp
from jax import lax
from jax.experimental import pallas as pl
from jax.experimental.pallas import tpu as pltpu
from jax.sharding import PartitionSpec as P

SIDES = 16
BLK = 256
KN = 16
BPD = 8
BLOCKS = BPD * KN
GROUPS = 8
INNER = 16
RANK = 32
LANES = 128
CAP = 3
KIND_ROWS = CAP * SIDES
NEAR_ROWS = 3 * KIND_ROWS
ROWS = NEAR_ROWS + 2 * SIDES
SUMS = BPD * SIDES
NOWHERE = 64
CHIPS = 4
PIECE = 16
F32 = jnp.float32
BF16 = jnp.bfloat16
I32 = jnp.int32


def away(place):
    return min(place, CHIPS - place)


INNER_ORDER = sorted(range(INNER), key=lambda i: (-away(i // CHIPS) - away(i % CHIPS), i))
OUTER_ORDER = sorted(range(GROUPS), key=lambda g: (-away(g // 2), g))


def rows_of(shape):
    return lax.broadcasted_iota(I32, shape, 0)


def lanes_of(shape):
    return lax.broadcasted_iota(I32, shape, len(shape) - 1)


def slot_of(cols, rank, group):
    apart = (cols >> 7) ^ group
    kind = jnp.where(apart == 0, 0, jnp.where(apart == 1, 1, 2))
    return kind * CAP + rank


def send_kernel(
    cols_hbm, cur_hbm, row_hbm, blocks_hbm, out_ref,
    cols_ref, cur_ref, row_ref, blocks_ref, place_ref, dest_ref, small_sem, block_sem,
):
    cols_copy = pltpu.make_async_copy(cols_hbm, cols_ref, small_sem.at[0])
    cur_copy = pltpu.make_async_copy(cur_hbm, cur_ref, small_sem.at[1])
    row_copy = pltpu.make_async_copy(row_hbm, row_ref, small_sem.at[2])
    dest_copy = pltpu.make_async_copy(place_ref, dest_ref, small_sem.at[3])
    cols_copy.start()
    cur_copy.start()
    row_copy.start()
    block_copies = []
    for c in range(BLOCKS // PIECE):
        part = pl.ds(c * PIECE, PIECE)
        copy = pltpu.make_async_copy(blocks_hbm.at[part], blocks_ref.at[part], block_sem.at[c])
        copy.start(priority=1)
        block_copies.append(copy)
    group = lax.axis_index("outer")
    for t in range(INNER):
        out_ref[t * ROWS : t * ROWS + NEAR_ROWS, :] = jnp.zeros((NEAR_ROWS, BLK), BF16)

    cols_copy.wait()
    table = cols_ref[...].astype(F32)
    spread = jnp.concatenate(
        [jnp.broadcast_to(table[b : b + 1, :], (KN, KN)) for b in range(BPD)], axis=0
    )
    shape = (BLOCKS, KN)
    picked = jnp.where(lanes_of(shape) == rows_of(shape) % KN, spread, 0.0)
    down = jnp.sum(picked, axis=1, keepdims=True)
    square = (BLOCKS, BLOCKS)
    wide = jnp.broadcast_to(down, square)
    across = wide.T[:1, :].astype(I32)
    down = down.astype(I32)
    same = (wide.astype(I32) >> 3) == (wide.T.astype(I32) >> 3)
    above = rows_of(square) < lanes_of(square)
    below = rows_of(square) > lanes_of(square)
    rank_across = jnp.sum(jnp.where(same & above, 1.0, 0.0), axis=0, keepdims=True).astype(I32)
    rank_down = jnp.sum(jnp.where(same & below, 1.0, 0.0), axis=1, keepdims=True).astype(I32)
    inner = (across >> 3) & (INNER - 1)
    target = jnp.zeros_like(inner)
    for position, device in enumerate(INNER_ORDER):
        target = jnp.where(inner == device, position, target)
    first_row = target * ROWS + slot_of(across, rank_across, group) * SIDES
    place_ref[...] = jnp.broadcast_to(first_row, place_ref.shape)
    dest_copy.start()
    to_target = jnp.where(rows_of((INNER, BLOCKS)) == target, 1.0, 0.0).astype(BF16)
    lane = group * RANK + slot_of(down, rank_down, group)
    block_id = ((down & (BPD - 1)) - NOWHERE).astype(F32)
    at_slot = jnp.where(lanes_of((BLOCKS, BLK)) == lane, block_id, 0.0).astype(BF16)
    ids = jnp.dot(to_target, at_slot, preferred_element_type=F32) + float(NOWHERE)

    cur_copy.wait()
    row_copy.wait()
    term = lax.dot_general(
        cur_ref[...], row_ref[...], (((1,), (1,)), ((), ())), preferred_element_type=F32
    )
    high = term.astype(BF16)
    low = term - high.astype(F32)
    own = lanes_of((SIDES, BLK)) // RANK == group
    for t in range(INNER):
        far_row = t * ROWS + NEAR_ROWS
        out_ref[far_row : far_row + SIDES, :] = high
        out_ref[far_row + SIDES : far_row + 2 * SIDES, :] = jnp.where(
            own, ids[t : t + 1, :], low
        ).astype(BF16)

    dest_copy.wait()
    for c in range(BLOCKS // PIECE):
        block_copies[c].wait()
        for e in range(c * PIECE, (c + 1) * PIECE):
            b = e // KN
            currents = cur_ref[:, b * BLK : (b + 1) * BLK]
            product = jnp.dot(currents, blocks_ref[e], preferred_element_type=F32)
            row = pl.multiple_of(dest_ref[0, e], SIDES)
            out_ref[pl.ds(row, SIDES), :] = product.astype(BF16)


def places_of(got_ref):
    group = lax.axis_index("outer")
    lows = got_ref[:, NEAR_ROWS + SIDES :, :].reshape(INNER * SIDES, BLK)
    square = (BLK, BLK)
    expand = rows_of(square) == group * RANK + lanes_of(square) // SIDES
    expand = jnp.where(expand, float(SIDES), 0.0).astype(BF16)
    places = jnp.dot(lows, expand, preferred_element_type=F32)
    lane = lanes_of((INNER * SIDES, BLK))
    return places + (lane % SIDES + lane // KIND_ROWS * SUMS).astype(F32)


def add_slots(got_ref, places, first_kind, kinds):
    start = first_kind * KIND_ROWS
    stop = start + kinds * KIND_ROWS
    rows = (rows_of((kinds * SUMS, stop - start)) + first_kind * SUMS).astype(F32)
    total = jnp.zeros((kinds * SUMS, BLK), F32)
    for i in range(INNER):
        place = places[i * SIDES : (i + 1) * SIDES, start:stop]
        pick = jnp.where(jnp.tile(place, (kinds * BPD, 1)) == rows, 1.0, 0.0).astype(BF16)
        total += jnp.dot(pick, got_ref[i, start:stop, :], preferred_element_type=F32)
    return total


def coef_kernel(got_ref, coef_ref):
    coef = jnp.zeros((SIDES, BLK), F32)
    for i in range(INNER):
        high = got_ref[i, :SIDES, :].astype(F32)
        low = got_ref[i, SIDES:, :].astype(F32)
        coef += high + low
    coef_ref[...] = jnp.zeros_like(coef_ref)
    for position, h in enumerate(OUTER_ORDER):
        coef_ref[position, :, :RANK] = coef[:, h * RANK : (h + 1) * RANK].astype(BF16)


def sum_kernel(got_ref, res_ref, cur_ref, after_ref, core_ref, next_ref, out_ref):
    del after_ref
    places = places_of(got_ref)
    total = add_slots(got_ref, places, 1, 2)
    core_ref[...] = total[:SUMS]
    next_ref[...] = total[SUMS:]
    total = add_slots(got_ref, places, 0, 1)
    for b in range(BPD):
        cut = slice(b * BLK, (b + 1) * BLK)
        diagonal = res_ref[:, cut] * cur_ref[:, cut].astype(F32)
        out_ref[:, cut] = diagonal + total[b * SIDES : (b + 1) * SIDES, :]


def final_kernel(coef_ref, col_ref, base_ref, core_ref, next_ref, out_ref):
    pieces = [coef_ref[OUTER_ORDER.index(g), :, :RANK] for g in range(GROUPS)]
    coef = jnp.concatenate(pieces, axis=1)
    own = lanes_of((SIDES, BLK)) // RANK == lax.axis_index("outer")
    coef = jnp.where(own, 0.0, coef.astype(F32)).astype(BF16)
    far = jnp.dot(coef, col_ref[...], preferred_element_type=F32)
    for b in range(BPD):
        cut = slice(b * BLK, (b + 1) * BLK)
        rows = slice(b * SIDES, (b + 1) * SIDES)
        near = base_ref[:, cut] + core_ref[rows, :] + next_ref[rows, :]
        out_ref[:, cut] = far[:, cut] + near


def params(mebibytes=12):
    return pltpu.CompilerParams(vmem_limit_bytes=mebibytes * 1024 * 1024)


def cost(flops, moved):
    return pl.CostEstimate(flops=flops, bytes_accessed=moved, transcendentals=0)


def exchange(array, axis, order):
    return lax.all_to_all(
        array, axis, split_axis=0, concat_axis=0, axis_index_groups=[order], tiled=True
    )


def in_hbm(array):
    return pltpu.with_memory_space_constraint(array, pltpu.HBM)


def on_device(currents, near_blocks, near_cols, row_factors, col_factors, resistance):
    filaments = currents.shape[1]
    flat = GROUPS * RANK
    in_vmem = pl.BlockSpec(memory_space=pltpu.VMEM)
    anywhere = pl.BlockSpec(memory_space=pl.ANY)

    payload = pl.pallas_call(
        send_kernel,
        out_shape=jax.ShapeDtypeStruct((INNER * ROWS, BLK), BF16),
        in_specs=[anywhere] * 4,
        out_specs=in_vmem,
        scratch_shapes=[
            pltpu.VMEM((BPD, KN), I32),
            pltpu.VMEM((SIDES, filaments), BF16),
            pltpu.VMEM((flat, filaments), BF16),
            pltpu.VMEM((BLOCKS, BLK, BLK), BF16),
            pltpu.VMEM((8, BLOCKS), I32),
            pltpu.SMEM((8, BLOCKS), I32),
            pltpu.SemaphoreType.DMA((4,)),
            pltpu.SemaphoreType.DMA((BLOCKS // PIECE,)),
        ],
        compiler_params=params(50),
        cost_estimate=cost(2 * BLOCKS * SIDES * BLK * BLK, 18000000),
    )(
        in_hbm(near_cols),
        in_hbm(currents),
        in_hbm(row_factors.reshape(flat, filaments)),
        in_hbm(near_blocks.reshape(BLOCKS, BLK, BLK)),
    )

    got = exchange(payload.reshape(INNER, ROWS, BLK), "inner", INNER_ORDER)

    coef = pl.pallas_call(
        coef_kernel,
        out_shape=jax.ShapeDtypeStruct((GROUPS, SIDES, LANES), BF16),
        compiler_params=params(),
        cost_estimate=cost(200000, 300000),
    )(got[:, NEAR_ROWS:, :])
    sums = jax.ShapeDtypeStruct((SUMS, BLK), F32)
    to_core, to_next, base = pl.pallas_call(
        sum_kernel,
        out_shape=(sums, sums, jax.ShapeDtypeStruct((SIDES, filaments), F32)),
        in_specs=[in_vmem] * 3 + [anywhere],
        compiler_params=params(),
        cost_estimate=cost(2 * 384 * 96 * 16 * 256, 2000000),
    )(got, resistance[None, :], currents, coef)
    core_pairs = [(g, g ^ 1) for g in range(GROUPS)]
    next_pairs = [(g, (g + (1 if g % 2 else -1)) % GROUPS) for g in range(GROUPS)]
    from_next = lax.ppermute(to_next, "outer", next_pairs)
    from_core = lax.ppermute(to_core, "outer", core_pairs)
    coef = exchange(coef, "outer", OUTER_ORDER)

    return pl.pallas_call(
        final_kernel,
        out_shape=jax.ShapeDtypeStruct((SIDES, filaments), F32),
        compiler_params=params(),
        cost_estimate=cost(2 * SIDES * flat * filaments, 1600000),
    )(coef, col_factors.reshape(flat, filaments), base, from_core, from_next)


def solution(mesh):
    return jax.shard_map(
        on_device,
        mesh=mesh,
        in_specs=(
            P(None, ("outer", "inner")),
            P(("outer", "inner"), None, None, None),
            P(("outer", "inner"), None),
            P(None, None, ("outer", "inner")),
            P(None, None, ("outer", "inner")),
            P(("outer", "inner")),
        ),
        out_specs=P(None, ("outer", "inner")),
        check_vma=False,
    )
```

```python
import jax
import jax.numpy as jnp
from jax import lax
from jax.experimental import pallas as pl
from jax.experimental.pallas import tpu as pltpu
from jax.sharding import PartitionSpec as P

SIDES = 16
BLK = 256
KN = 16
BPD = 8
BLOCKS = BPD * KN
GROUPS = 8
INNER = 16
RANK = 32
LANES = 128
CAP = 3
KIND_ROWS = CAP * SIDES
NEAR_ROWS = 3 * KIND_ROWS
ROWS = NEAR_ROWS + 2 * SIDES
SUMS = BPD * SIDES
NOWHERE = 64
CHIPS = 4
PIECE = 8
F32 = jnp.float32
BF16 = jnp.bfloat16
I32 = jnp.int32


def away(place):
    return min(place, CHIPS - place)


INNER_ORDER = sorted(range(INNER), key=lambda i: (-away(i // CHIPS) - away(i % CHIPS), i))
OUTER_ORDER = sorted(range(GROUPS), key=lambda g: (g % 2 == 0, -away(g // 2), -g))


def rows_of(shape):
    return lax.broadcasted_iota(I32, shape, 0)


def lanes_of(shape):
    return lax.broadcasted_iota(I32, shape, len(shape) - 1)


def slot_of(cols, rank, group):
    apart = (cols >> 7) ^ group
    kind = jnp.where(apart == 0, 0, jnp.where(apart == 1, 1, 2))
    return kind * CAP + rank


def send_kernel(
    cols_hbm, cur_hbm, row_hbm, blocks_hbm, out_ref,
    cols_ref, cur_ref, row_ref, blocks_ref, place_ref, dest_ref, small_sem, block_sem,
):
    cols_copy = pltpu.make_async_copy(cols_hbm, cols_ref, small_sem.at[0])
    cur_copy = pltpu.make_async_copy(cur_hbm, cur_ref, small_sem.at[1])
    row_copy = pltpu.make_async_copy(row_hbm, row_ref, small_sem.at[2])
    dest_copy = pltpu.make_async_copy(place_ref, dest_ref, small_sem.at[3])
    cols_copy.start()
    cur_copy.start()
    row_copy.start()
    block_copies = []
    for c in range(BLOCKS // PIECE):
        part = pl.ds(c * PIECE, PIECE)
        copy = pltpu.make_async_copy(blocks_hbm.at[part], blocks_ref.at[part], block_sem.at[c])
        copy.start(priority=1)
        block_copies.append(copy)
    group = lax.axis_index("outer")
    for t in range(INNER):
        out_ref[t * ROWS : t * ROWS + NEAR_ROWS, :] = jnp.zeros((NEAR_ROWS, BLK), BF16)

    cols_copy.wait()
    table = cols_ref[...].astype(F32)
    spread = jnp.concatenate(
        [jnp.broadcast_to(table[b : b + 1, :], (KN, KN)) for b in range(BPD)], axis=0
    )
    shape = (BLOCKS, KN)
    picked = jnp.where(lanes_of(shape) == rows_of(shape) % KN, spread, 0.0)
    down = jnp.sum(picked, axis=1, keepdims=True)
    square = (BLOCKS, BLOCKS)
    wide = jnp.broadcast_to(down, square)
    across = wide.T[:1, :].astype(I32)
    down = down.astype(I32)
    same = (wide.astype(I32) >> 3) == (wide.T.astype(I32) >> 3)
    above = rows_of(square) < lanes_of(square)
    below = rows_of(square) > lanes_of(square)
    rank_across = jnp.sum(jnp.where(same & above, 1.0, 0.0), axis=0, keepdims=True).astype(I32)
    rank_down = jnp.sum(jnp.where(same & below, 1.0, 0.0), axis=1, keepdims=True).astype(I32)
    inner = (across >> 3) & (INNER - 1)
    target = jnp.zeros_like(inner)
    for position, device in enumerate(INNER_ORDER):
        target = jnp.where(inner == device, position, target)
    first_row = target * ROWS + slot_of(across, rank_across, group) * SIDES
    place_ref[...] = jnp.broadcast_to(first_row, place_ref.shape)
    dest_copy.start()
    to_target = jnp.where(rows_of((INNER, BLOCKS)) == target, 1.0, 0.0).astype(BF16)
    lane = group * RANK + slot_of(down, rank_down, group)
    block_id = ((down & (BPD - 1)) - NOWHERE).astype(F32)
    at_slot = jnp.where(lanes_of((BLOCKS, BLK)) == lane, block_id, 0.0).astype(BF16)
    ids = jnp.dot(to_target, at_slot, preferred_element_type=F32) + float(NOWHERE)

    cur_copy.wait()
    row_copy.wait()
    term = lax.dot_general(
        cur_ref[...], row_ref[...], (((1,), (1,)), ((), ())), preferred_element_type=F32
    )
    high = term.astype(BF16)
    low = term - high.astype(F32)
    own = lanes_of((SIDES, BLK)) // RANK == group
    for t in range(INNER):
        far_row = t * ROWS + NEAR_ROWS
        out_ref[far_row : far_row + SIDES, :] = high
        out_ref[far_row + SIDES : far_row + 2 * SIDES, :] = jnp.where(
            own, ids[t : t + 1, :], low
        ).astype(BF16)

    dest_copy.wait()
    for c in range(BLOCKS // PIECE):
        block_copies[c].wait()
        for e in range(c * PIECE, (c + 1) * PIECE):
            b = e // KN
            currents = cur_ref[:, b * BLK : (b + 1) * BLK]
            product = jnp.dot(currents, blocks_ref[e], preferred_element_type=F32)
            row = pl.multiple_of(dest_ref[0, e], SIDES)
            out_ref[pl.ds(row, SIDES), :] = product.astype(BF16)


def add_slots(got_ref, first_kind, kinds):
    start = first_kind * KIND_ROWS
    first_lane = lax.axis_index("outer") * RANK + first_kind * CAP
    lows = got_ref[:, NEAR_ROWS + SIDES :, :].reshape(INNER * SIDES, BLK)
    shape = (BLK, LANES)
    expand = rows_of(shape) == first_lane + lanes_of(shape) // SIDES
    expand = jnp.where(expand, float(SIDES), 0.0).astype(BF16)
    lane = lanes_of((INNER * SIDES, LANES))
    shift = lane % SIDES + lane // KIND_ROWS * SUMS
    shift = jnp.where(lane < kinds * KIND_ROWS, shift, 3 * SUMS).astype(F32)
    places = jnp.dot(lows, expand, preferred_element_type=F32) + shift
    rows = rows_of((kinds * SUMS, LANES)).astype(F32)
    total = jnp.zeros((kinds * SUMS, BLK), F32)
    for i in range(0, INNER, 2):
        picks, slots = [], []
        for j in (i, i + 1):
            place = jnp.tile(places[j * SIDES : (j + 1) * SIDES], (kinds * BPD, 1))
            picks.append(jnp.where(place == rows, 1.0, 0.0).astype(BF16))
            slots.append(got_ref[j, start : start + LANES, :])
        pick, slot = jnp.concatenate(picks, axis=1), jnp.concatenate(slots, axis=0)
        total += jnp.dot(pick, slot, preferred_element_type=F32)
    return total


def coef_kernel(got_ref, coef_ref):
    coef = jnp.zeros((SIDES, BLK), F32)
    for i in range(INNER):
        high = got_ref[i, :SIDES, :].astype(F32)
        low = got_ref[i, SIDES:, :].astype(F32)
        coef += high + low
    coef_ref[...] = jnp.zeros_like(coef_ref)
    for position, h in enumerate(OUTER_ORDER):
        coef_ref[position, :, :RANK] = coef[:, h * RANK : (h + 1) * RANK].astype(BF16)


def sum_kernel(got_ref, res_ref, cur_ref, after_ref, core_ref, next_ref, out_ref):
    del after_ref
    total = add_slots(got_ref, 1, 2)
    core_ref[...] = total[:SUMS]
    next_ref[...] = total[SUMS:]
    total = add_slots(got_ref, 0, 1)
    for b in range(BPD):
        cut = slice(b * BLK, (b + 1) * BLK)
        diagonal = res_ref[:, cut] * cur_ref[:, cut].astype(F32)
        out_ref[:, cut] = diagonal + total[b * SIDES : (b + 1) * SIDES, :]


def final_kernel(coef_ref, col_ref, base_ref, core_ref, next_ref, out_ref):
    pieces = [coef_ref[OUTER_ORDER.index(g), :, :RANK] for g in range(GROUPS)]
    coef = jnp.concatenate(pieces, axis=1)
    own = lanes_of((SIDES, BLK)) // RANK == lax.axis_index("outer")
    coef = jnp.where(own, 0.0, coef.astype(F32)).astype(BF16)
    far = jnp.dot(coef, col_ref[...], preferred_element_type=F32)
    for b in range(BPD):
        cut = slice(b * BLK, (b + 1) * BLK)
        rows = slice(b * SIDES, (b + 1) * SIDES)
        near = base_ref[:, cut] + core_ref[rows, :] + next_ref[rows, :]
        out_ref[:, cut] = far[:, cut] + near


def params(mebibytes=12):
    return pltpu.CompilerParams(vmem_limit_bytes=mebibytes * 1024 * 1024)


def cost(flops, moved):
    return pl.CostEstimate(flops=flops, bytes_accessed=moved, transcendentals=0)


def exchange(array, axis, order):
    return lax.all_to_all(
        array, axis, split_axis=0, concat_axis=0, axis_index_groups=[order], tiled=True
    )


def in_hbm(array):
    return pltpu.with_memory_space_constraint(array, pltpu.HBM)


def on_device(currents, near_blocks, near_cols, row_factors, col_factors, resistance):
    filaments = currents.shape[1]
    flat = GROUPS * RANK
    in_vmem = pl.BlockSpec(memory_space=pltpu.VMEM)
    anywhere = pl.BlockSpec(memory_space=pl.ANY)

    payload = pl.pallas_call(
        send_kernel,
        out_shape=jax.ShapeDtypeStruct((INNER * ROWS, BLK), BF16),
        in_specs=[anywhere] * 4,
        out_specs=in_vmem,
        scratch_shapes=[
            pltpu.VMEM((BPD, KN), I32),
            pltpu.VMEM((SIDES, filaments), BF16),
            pltpu.VMEM((flat, filaments), BF16),
            pltpu.VMEM((BLOCKS, BLK, BLK), BF16),
            pltpu.VMEM((8, BLOCKS), I32),
            pltpu.SMEM((8, BLOCKS), I32),
            pltpu.SemaphoreType.DMA((4,)),
            pltpu.SemaphoreType.DMA((BLOCKS // PIECE,)),
        ],
        compiler_params=params(50),
        cost_estimate=cost(2 * BLOCKS * SIDES * BLK * BLK, 18000000),
    )(
        in_hbm(near_cols),
        in_hbm(currents),
        in_hbm(row_factors.reshape(flat, filaments)),
        in_hbm(near_blocks.reshape(BLOCKS, BLK, BLK)),
    )

    got = exchange(payload.reshape(INNER, ROWS, BLK), "inner", INNER_ORDER)

    coef = pl.pallas_call(
        coef_kernel,
        out_shape=jax.ShapeDtypeStruct((GROUPS, SIDES, LANES), BF16),
        compiler_params=params(),
        cost_estimate=cost(200000, 300000),
    )(got[:, NEAR_ROWS:, :])
    sums = jax.ShapeDtypeStruct((SUMS, BLK), F32)
    to_core, to_next, base = pl.pallas_call(
        sum_kernel,
        out_shape=(sums, sums, jax.ShapeDtypeStruct((SIDES, filaments), F32)),
        in_specs=[in_vmem] * 3 + [anywhere],
        compiler_params=params(),
        cost_estimate=cost(2 * 384 * 96 * 16 * 256, 2000000),
    )(got, resistance[None, :], currents, coef)
    core_pairs = [(g, g ^ 1) for g in range(GROUPS)]
    next_pairs = [(g, (g + (1 if g % 2 else -1)) % GROUPS) for g in range(GROUPS)]
    from_next = lax.ppermute(to_next, "outer", next_pairs)
    from_core = lax.ppermute(to_core, "outer", core_pairs)
    coef = exchange(coef, "outer", OUTER_ORDER)

    return pl.pallas_call(
        final_kernel,
        out_shape=jax.ShapeDtypeStruct((SIDES, filaments), F32),
        compiler_params=params(),
        cost_estimate=cost(2 * SIDES * flat * filaments, 1600000),
    )(coef, col_factors.reshape(flat, filaments), base, from_core, from_next)


def solution(mesh):
    return jax.shard_map(
        on_device,
        mesh=mesh,
        in_specs=(
            P(None, ("outer", "inner")),
            P(("outer", "inner"), None, None, None),
            P(("outer", "inner"), None),
            P(None, None, ("outer", "inner")),
            P(None, None, ("outer", "inner")),
            P(("outer", "inner")),
        ),
        out_specs=P(None, ("outer", "inner")),
        check_vma=False,
    )
```

```python
import jax
import jax.numpy as jnp
from jax import lax
from jax.experimental import pallas as pl
from jax.experimental.pallas import tpu as pltpu
from jax.sharding import PartitionSpec as P

SIDES = 16
BLK = 256
KN = 16
BPD = 8
BLOCKS = BPD * KN
GROUPS = 8
INNER = 16
RANK = 32
LANES = 128
CAP = 3
KIND_ROWS = CAP * SIDES
NEAR_ROWS = 3 * KIND_ROWS
ROWS = NEAR_ROWS + 2 * SIDES
SUMS = BPD * SIDES
NOWHERE = 64
CHIPS = 4
PIECE = 8
F32 = jnp.float32
BF16 = jnp.bfloat16
I32 = jnp.int32


def away(place):
    return min(place, CHIPS - place)


INNER_ORDER = sorted(range(INNER), key=lambda i: (-away(i // CHIPS) - away(i % CHIPS), i))
OUTER_ORDER = sorted(range(GROUPS), key=lambda g: (g % 2 == 0, -away(g // 2), -g))


def rows_of(shape):
    return lax.broadcasted_iota(I32, shape, 0)


def lanes_of(shape):
    return lax.broadcasted_iota(I32, shape, len(shape) - 1)


def slot_of(cols, rank, group):
    apart = (cols >> 7) ^ group
    kind = jnp.where(apart == 0, 0, jnp.where(apart == 1, 1, 2))
    return kind * CAP + rank


def send_kernel(
    cols_hbm, cur_hbm, row_hbm, blocks_hbm, out_ref,
    cols_ref, cur_ref, row_ref, blocks_ref, place_ref, dest_ref, small_sem, block_sem,
):
    cols_copy = pltpu.make_async_copy(cols_hbm, cols_ref, small_sem.at[0])
    cur_copy = pltpu.make_async_copy(cur_hbm, cur_ref, small_sem.at[1])
    row_copy = pltpu.make_async_copy(row_hbm, row_ref, small_sem.at[2])
    dest_copy = pltpu.make_async_copy(place_ref, dest_ref, small_sem.at[3])
    cols_copy.start()
    cur_copy.start()
    row_copy.start()
    block_copies = []
    for c in range(BLOCKS // PIECE):
        part = pl.ds(c * PIECE, PIECE)
        copy = pltpu.make_async_copy(blocks_hbm.at[part], blocks_ref.at[part], block_sem.at[c])
        copy.start(priority=1)
        block_copies.append(copy)
    group = lax.axis_index("outer")
    for t in range(INNER):
        out_ref[t * ROWS : t * ROWS + NEAR_ROWS, :] = jnp.zeros((NEAR_ROWS, BLK), BF16)

    cols_copy.wait()
    table = cols_ref[...].astype(F32)
    spread = jnp.concatenate(
        [jnp.broadcast_to(table[b : b + 1, :], (KN, KN)) for b in range(BPD)], axis=0
    )
    shape = (BLOCKS, KN)
    picked = jnp.where(lanes_of(shape) == rows_of(shape) % KN, spread, 0.0)
    down = jnp.sum(picked, axis=1, keepdims=True)
    square = (BLOCKS, BLOCKS)
    wide = jnp.broadcast_to(down, square)
    across = wide.T[:1, :].astype(I32)
    down = down.astype(I32)
    same = (wide.astype(I32) >> 3) == (wide.T.astype(I32) >> 3)
    above = rows_of(square) < lanes_of(square)
    below = rows_of(square) > lanes_of(square)
    rank_across = jnp.sum(jnp.where(same & above, 1.0, 0.0), axis=0, keepdims=True).astype(I32)
    rank_down = jnp.sum(jnp.where(same & below, 1.0, 0.0), axis=1, keepdims=True).astype(I32)
    inner = (across >> 3) & (INNER - 1)
    target = jnp.zeros_like(inner)
    for position, device in enumerate(INNER_ORDER):
        target = jnp.where(inner == device, position, target)
    first_row = target * ROWS + slot_of(across, rank_across, group) * SIDES
    place_ref[...] = jnp.broadcast_to(first_row, place_ref.shape)
    dest_copy.start()
    to_target = jnp.where(rows_of((INNER, BLOCKS)) == target, 1.0, 0.0).astype(BF16)
    lane = group * RANK + slot_of(down, rank_down, group)
    block_id = ((down & (BPD - 1)) - NOWHERE).astype(F32)
    at_slot = jnp.where(lanes_of((BLOCKS, BLK)) == lane, block_id, 0.0).astype(BF16)
    ids = jnp.dot(to_target, at_slot, preferred_element_type=F32) + float(NOWHERE)

    cur_copy.wait()
    row_copy.wait()
    term = lax.dot_general(
        cur_ref[...], row_ref[...], (((1,), (1,)), ((), ())), preferred_element_type=F32
    )
    high = term.astype(BF16)
    low = term - high.astype(F32)
    own = lanes_of((SIDES, BLK)) // RANK == group
    for t in range(INNER):
        far_row = t * ROWS + NEAR_ROWS
        out_ref[far_row : far_row + SIDES, :] = high
        out_ref[far_row + SIDES : far_row + 2 * SIDES, :] = jnp.where(
            own, ids[t : t + 1, :], low
        ).astype(BF16)

    dest_copy.wait()
    for c in range(BLOCKS // PIECE):
        block_copies[c].wait()
        for e in range(c * PIECE, (c + 1) * PIECE):
            b = e // KN
            currents = cur_ref[:, b * BLK : (b + 1) * BLK]
            product = jnp.dot(currents, blocks_ref[e], preferred_element_type=F32)
            row = pl.multiple_of(dest_ref[0, e], SIDES)
            out_ref[pl.ds(row, SIDES), :] = product.astype(BF16)


def add_slots(got_ref, first_kind, kinds):
    start = first_kind * KIND_ROWS
    first_lane = lax.axis_index("outer") * RANK + first_kind * CAP
    lows = got_ref[:, NEAR_ROWS + SIDES :, :].reshape(INNER * SIDES, BLK)
    shape = (BLK, LANES)
    expand = rows_of(shape) == first_lane + lanes_of(shape) // SIDES
    expand = jnp.where(expand, float(SIDES), 0.0).astype(BF16)
    lane = lanes_of((INNER * SIDES, LANES))
    shift = lane % SIDES + lane // KIND_ROWS * SUMS
    shift = jnp.where(lane < kinds * KIND_ROWS, shift, 3 * SUMS).astype(F32)
    places = jnp.dot(lows, expand, preferred_element_type=F32) + shift
    rows = rows_of((kinds * SUMS, LANES)).astype(F32)
    total = jnp.zeros((kinds * SUMS, BLK), F32)
    for i in range(0, INNER, 2):
        picks, slots = [], []
        for j in (i, i + 1):
            place = jnp.tile(places[j * SIDES : (j + 1) * SIDES], (kinds * BPD, 1))
            picks.append(jnp.where(place == rows, 1.0, 0.0).astype(BF16))
            slots.append(got_ref[j, start : start + LANES, :])
        pick, slot = jnp.concatenate(picks, axis=1), jnp.concatenate(slots, axis=0)
        total += jnp.dot(pick, slot, preferred_element_type=F32)
    return total


def coef_kernel(got_ref, coef_ref):
    coef = jnp.zeros((SIDES, BLK), F32)
    for i in range(INNER):
        high = got_ref[i, :SIDES, :].astype(F32)
        low = got_ref[i, SIDES:, :].astype(F32)
        coef += high + low
    coef_ref[...] = jnp.zeros_like(coef_ref)
    for position, h in enumerate(OUTER_ORDER):
        coef_ref[position, :, :RANK] = coef[:, h * RANK : (h + 1) * RANK].astype(BF16)


def sum_kernel(got_ref, res_ref, cur_ref, core_ref, next_ref, out_ref):
    total = add_slots(got_ref, 1, 2)
    core_ref[...] = total[:SUMS]
    next_ref[...] = total[SUMS:]
    total = add_slots(got_ref, 0, 1)
    for b in range(BPD):
        cut = slice(b * BLK, (b + 1) * BLK)
        diagonal = res_ref[:, cut] * cur_ref[:, cut].astype(F32)
        out_ref[:, cut] = diagonal + total[b * SIDES : (b + 1) * SIDES, :]


def final_kernel(coef_ref, col_ref, base_ref, core_ref, next_ref, out_ref):
    pieces = [coef_ref[OUTER_ORDER.index(g), :, :RANK] for g in range(GROUPS)]
    coef = jnp.concatenate(pieces, axis=1)
    own = lanes_of((SIDES, BLK)) // RANK == lax.axis_index("outer")
    coef = jnp.where(own, 0.0, coef.astype(F32)).astype(BF16)
    far = jnp.dot(coef, col_ref[...], preferred_element_type=F32)
    for b in range(BPD):
        cut = slice(b * BLK, (b + 1) * BLK)
        rows = slice(b * SIDES, (b + 1) * SIDES)
        near = base_ref[:, cut] + core_ref[rows, :] + next_ref[rows, :]
        out_ref[:, cut] = far[:, cut] + near


def params(mebibytes=12):
    return pltpu.CompilerParams(vmem_limit_bytes=mebibytes * 1024 * 1024)


def cost(flops, moved):
    return pl.CostEstimate(flops=flops, bytes_accessed=moved, transcendentals=0)


def exchange(array, axis, order):
    return lax.all_to_all(
        array, axis, split_axis=0, concat_axis=0, axis_index_groups=[order], tiled=True
    )


def in_hbm(array):
    return pltpu.with_memory_space_constraint(array, pltpu.HBM)


def on_device(currents, near_blocks, near_cols, row_factors, col_factors, resistance):
    filaments = currents.shape[1]
    flat = GROUPS * RANK
    in_vmem = pl.BlockSpec(memory_space=pltpu.VMEM)
    anywhere = pl.BlockSpec(memory_space=pl.ANY)

    payload = pl.pallas_call(
        send_kernel,
        out_shape=jax.ShapeDtypeStruct((INNER * ROWS, BLK), BF16),
        in_specs=[anywhere] * 4,
        out_specs=in_vmem,
        scratch_shapes=[
            pltpu.VMEM((BPD, KN), I32),
            pltpu.VMEM((SIDES, filaments), BF16),
            pltpu.VMEM((flat, filaments), BF16),
            pltpu.VMEM((BLOCKS, BLK, BLK), BF16),
            pltpu.VMEM((8, BLOCKS), I32),
            pltpu.SMEM((8, BLOCKS), I32),
            pltpu.SemaphoreType.DMA((4,)),
            pltpu.SemaphoreType.DMA((BLOCKS // PIECE,)),
        ],
        compiler_params=params(50),
        cost_estimate=cost(2 * BLOCKS * SIDES * BLK * BLK, 18000000),
    )(
        in_hbm(near_cols),
        in_hbm(currents),
        in_hbm(row_factors.reshape(flat, filaments)),
        in_hbm(near_blocks.reshape(BLOCKS, BLK, BLK)),
    )

    got = exchange(payload.reshape(INNER, ROWS, BLK), "inner", INNER_ORDER)

    coef = pl.pallas_call(
        coef_kernel,
        out_shape=jax.ShapeDtypeStruct((GROUPS, SIDES, LANES), BF16),
        compiler_params=params(),
        cost_estimate=cost(200000, 300000),
    )(got[:, NEAR_ROWS:, :])
    sums = jax.ShapeDtypeStruct((SUMS, BLK), F32)
    to_core, to_next, base = pl.pallas_call(
        sum_kernel,
        out_shape=(sums, sums, jax.ShapeDtypeStruct((SIDES, filaments), F32)),
        in_specs=[in_vmem] * 3,
        compiler_params=params(),
        cost_estimate=cost(2 * 384 * 96 * 16 * 256, 2000000),
    )(got, resistance[None, :], currents)
    core_pairs = [(g, g ^ 1) for g in range(GROUPS)]
    next_pairs = [(g, (g + (1 if g % 2 else -1)) % GROUPS) for g in range(GROUPS)]
    from_next = lax.ppermute(to_next, "outer", next_pairs)
    from_core = lax.ppermute(to_core, "outer", core_pairs)
    coef = exchange(coef, "outer", OUTER_ORDER)

    return pl.pallas_call(
        final_kernel,
        out_shape=jax.ShapeDtypeStruct((SIDES, filaments), F32),
        compiler_params=params(),
        cost_estimate=cost(2 * SIDES * flat * filaments, 1600000),
    )(coef, col_factors.reshape(flat, filaments), base, from_core, from_next)


def solution(mesh):
    return jax.shard_map(
        on_device,
        mesh=mesh,
        in_specs=(
            P(None, ("outer", "inner")),
            P(("outer", "inner"), None, None, None),
            P(("outer", "inner"), None),
            P(None, None, ("outer", "inner")),
            P(None, None, ("outer", "inner")),
            P(("outer", "inner")),
        ),
        out_specs=P(None, ("outer", "inner")),
        check_vma=False,
    )
```

```python
import jax
import jax.numpy as jnp
from jax import lax
from jax.experimental import pallas as pl
from jax.experimental.pallas import tpu as pltpu
from jax.sharding import PartitionSpec as P

SIDES = 16
BLK = 256
KN = 16
BPD = 8
BLOCKS = BPD * KN
GROUPS = 8
INNER = 16
RANK = 32
LANES = 128
CAP = 3
KIND_ROWS = CAP * SIDES
NEAR_ROWS = 3 * KIND_ROWS
ROWS = NEAR_ROWS + 2 * SIDES
SUMS = BPD * SIDES
NOWHERE = 64
PIECE = 8
F32 = jnp.float32
BF16 = jnp.bfloat16
I32 = jnp.int32


INNER_ORDER = [10, 2, 7, 6, 1, 5, 15, 11, 14, 3, 12, 0, 9, 4, 13, 8]
OUTER_ORDER = [5, 3, 7, 1, 4, 2, 6, 0]


def rows_of(shape):
    return lax.broadcasted_iota(I32, shape, 0)


def lanes_of(shape):
    return lax.broadcasted_iota(I32, shape, len(shape) - 1)


def slot_of(cols, rank, group):
    apart = (cols >> 7) ^ group
    kind = jnp.where(apart == 0, 0, jnp.where(apart == 1, 1, 2))
    return kind * CAP + rank


def send_kernel(
    cols_hbm, cur_hbm, row_hbm, blocks_hbm, out_ref,
    cols_ref, cur_ref, row_ref, blocks_ref, place_ref, dest_ref, small_sem, block_sem,
):
    cols_copy = pltpu.make_async_copy(cols_hbm, cols_ref, small_sem.at[0])
    cur_copy = pltpu.make_async_copy(cur_hbm, cur_ref, small_sem.at[1])
    row_copy = pltpu.make_async_copy(row_hbm, row_ref, small_sem.at[2])
    dest_copy = pltpu.make_async_copy(place_ref, dest_ref, small_sem.at[3])
    cols_copy.start()
    cur_copy.start()
    row_copy.start()
    block_copies = []
    for c in range(BLOCKS // PIECE):
        part = pl.ds(c * PIECE, PIECE)
        copy = pltpu.make_async_copy(blocks_hbm.at[part], blocks_ref.at[part], block_sem.at[c])
        copy.start(priority=1)
        block_copies.append(copy)
    group = lax.axis_index("outer")
    for t in range(INNER):
        out_ref[t * ROWS : t * ROWS + NEAR_ROWS, :] = jnp.zeros((NEAR_ROWS, BLK), BF16)

    cols_copy.wait()
    table = cols_ref[...].astype(F32)
    spread = jnp.concatenate(
        [jnp.broadcast_to(table[b : b + 1, :], (KN, KN)) for b in range(BPD)], axis=0
    )
    shape = (BLOCKS, KN)
    picked = jnp.where(lanes_of(shape) == rows_of(shape) % KN, spread, 0.0)
    down = jnp.sum(picked, axis=1, keepdims=True)
    square = (BLOCKS, BLOCKS)
    wide = jnp.broadcast_to(down, square)
    across = wide.T[:1, :].astype(I32)
    down = down.astype(I32)
    same = (wide.astype(I32) >> 3) == (wide.T.astype(I32) >> 3)
    above = rows_of(square) < lanes_of(square)
    below = rows_of(square) > lanes_of(square)
    rank_across = jnp.sum(jnp.where(same & above, 1.0, 0.0), axis=0, keepdims=True).astype(I32)
    rank_down = jnp.sum(jnp.where(same & below, 1.0, 0.0), axis=1, keepdims=True).astype(I32)
    inner = (across >> 3) & (INNER - 1)
    target = jnp.zeros_like(inner)
    for position, device in enumerate(INNER_ORDER):
        target = jnp.where(inner == device, position, target)
    first_row = target * ROWS + slot_of(across, rank_across, group) * SIDES
    place_ref[...] = jnp.broadcast_to(first_row, place_ref.shape)
    dest_copy.start()
    to_target = jnp.where(rows_of((INNER, BLOCKS)) == target, 1.0, 0.0).astype(BF16)
    lane = group * RANK + slot_of(down, rank_down, group)
    block_id = ((down & (BPD - 1)) - NOWHERE).astype(F32)
    at_slot = jnp.where(lanes_of((BLOCKS, BLK)) == lane, block_id, 0.0).astype(BF16)
    ids = jnp.dot(to_target, at_slot, preferred_element_type=F32) + float(NOWHERE)

    cur_copy.wait()
    row_copy.wait()
    term = lax.dot_general(
        cur_ref[...], row_ref[...], (((1,), (1,)), ((), ())), preferred_element_type=F32
    )
    high = term.astype(BF16)
    low = term - high.astype(F32)
    own = lanes_of((SIDES, BLK)) // RANK == group
    for t in range(INNER):
        far_row = t * ROWS + NEAR_ROWS
        out_ref[far_row : far_row + SIDES, :] = high
        out_ref[far_row + SIDES : far_row + 2 * SIDES, :] = jnp.where(
            own, ids[t : t + 1, :], low
        ).astype(BF16)

    dest_copy.wait()
    for c in range(BLOCKS // PIECE):
        block_copies[c].wait()
        for e in range(c * PIECE, (c + 1) * PIECE):
            b = e // KN
            currents = cur_ref[:, b * BLK : (b + 1) * BLK]
            product = jnp.dot(currents, blocks_ref[e], preferred_element_type=F32)
            row = pl.multiple_of(dest_ref[0, e], SIDES)
            out_ref[pl.ds(row, SIDES), :] = product.astype(BF16)


def add_slots(got_ref, first_kind, kinds):
    start = first_kind * KIND_ROWS
    first_lane = lax.axis_index("outer") * RANK + first_kind * CAP
    lows = got_ref[:, NEAR_ROWS + SIDES :, :].reshape(INNER * SIDES, BLK)
    shape = (BLK, LANES)
    expand = rows_of(shape) == first_lane + lanes_of(shape) // SIDES
    expand = jnp.where(expand, float(SIDES), 0.0).astype(BF16)
    lane = lanes_of((INNER * SIDES, LANES))
    shift = lane % SIDES + lane // KIND_ROWS * SUMS
    shift = jnp.where(lane < kinds * KIND_ROWS, shift, 3 * SUMS).astype(F32)
    places = jnp.dot(lows, expand, preferred_element_type=F32) + shift
    rows = rows_of((kinds * SUMS, LANES)).astype(F32)
    total = jnp.zeros((kinds * SUMS, BLK), F32)
    for i in range(0, INNER, 2):
        picks, slots = [], []
        for j in (i, i + 1):
            place = jnp.tile(places[j * SIDES : (j + 1) * SIDES], (kinds * BPD, 1))
            picks.append(jnp.where(place == rows, 1.0, 0.0).astype(BF16))
            slots.append(got_ref[j, start : start + LANES, :])
        pick, slot = jnp.concatenate(picks, axis=1), jnp.concatenate(slots, axis=0)
        total += jnp.dot(pick, slot, preferred_element_type=F32)
    return total


def coef_kernel(got_ref, coef_ref):
    coef = jnp.zeros((SIDES, BLK), F32)
    for i in range(INNER):
        high = got_ref[i, :SIDES, :].astype(F32)
        low = got_ref[i, SIDES:, :].astype(F32)
        coef += high + low
    coef_ref[...] = jnp.zeros_like(coef_ref)
    for position, h in enumerate(OUTER_ORDER):
        coef_ref[position, :, :RANK] = coef[:, h * RANK : (h + 1) * RANK].astype(BF16)


def sum_kernel(got_ref, res_ref, cur_ref, core_ref, next_ref, out_ref):
    total = add_slots(got_ref, 1, 2)
    core_ref[...] = total[:SUMS]
    next_ref[...] = total[SUMS:]
    total = add_slots(got_ref, 0, 1)
    for b in range(BPD):
        cut = slice(b * BLK, (b + 1) * BLK)
        diagonal = res_ref[:, cut] * cur_ref[:, cut].astype(F32)
        out_ref[:, cut] = diagonal + total[b * SIDES : (b + 1) * SIDES, :]


def final_kernel(coef_ref, col_ref, base_ref, core_ref, next_ref, out_ref):
    pieces = [coef_ref[OUTER_ORDER.index(g), :, :RANK] for g in range(GROUPS)]
    coef = jnp.concatenate(pieces, axis=1)
    own = lanes_of((SIDES, BLK)) // RANK == lax.axis_index("outer")
    coef = jnp.where(own, 0.0, coef.astype(F32)).astype(BF16)
    far = jnp.dot(coef, col_ref[...], preferred_element_type=F32)
    for b in range(BPD):
        cut = slice(b * BLK, (b + 1) * BLK)
        rows = slice(b * SIDES, (b + 1) * SIDES)
        near = base_ref[:, cut] + core_ref[rows, :] + next_ref[rows, :]
        out_ref[:, cut] = far[:, cut] + near


def params(mebibytes=12):
    return pltpu.CompilerParams(vmem_limit_bytes=mebibytes * 1024 * 1024)


def cost(flops, moved):
    return pl.CostEstimate(flops=flops, bytes_accessed=moved, transcendentals=0)


def exchange(array, axis, order):
    return lax.all_to_all(
        array, axis, split_axis=0, concat_axis=0, axis_index_groups=[order], tiled=True
    )


def in_hbm(array):
    return pltpu.with_memory_space_constraint(array, pltpu.HBM)


def on_device(currents, near_blocks, near_cols, row_factors, col_factors, resistance):
    filaments = currents.shape[1]
    flat = GROUPS * RANK
    in_vmem = pl.BlockSpec(memory_space=pltpu.VMEM)
    anywhere = pl.BlockSpec(memory_space=pl.ANY)

    payload = pl.pallas_call(
        send_kernel,
        out_shape=jax.ShapeDtypeStruct((INNER * ROWS, BLK), BF16),
        in_specs=[anywhere] * 4,
        out_specs=in_vmem,
        scratch_shapes=[
            pltpu.VMEM((BPD, KN), I32),
            pltpu.VMEM((SIDES, filaments), BF16),
            pltpu.VMEM((flat, filaments), BF16),
            pltpu.VMEM((BLOCKS, BLK, BLK), BF16),
            pltpu.VMEM((8, BLOCKS), I32),
            pltpu.SMEM((8, BLOCKS), I32),
            pltpu.SemaphoreType.DMA((4,)),
            pltpu.SemaphoreType.DMA((BLOCKS // PIECE,)),
        ],
        compiler_params=params(50),
        cost_estimate=cost(2 * BLOCKS * SIDES * BLK * BLK, 18000000),
    )(
        in_hbm(near_cols),
        in_hbm(currents),
        in_hbm(row_factors.reshape(flat, filaments)),
        in_hbm(near_blocks.reshape(BLOCKS, BLK, BLK)),
    )

    got = exchange(payload.reshape(INNER, ROWS, BLK), "inner", INNER_ORDER)

    coef = pl.pallas_call(
        coef_kernel,
        out_shape=jax.ShapeDtypeStruct((GROUPS, SIDES, LANES), BF16),
        compiler_params=params(),
        cost_estimate=cost(200000, 300000),
    )(got[:, NEAR_ROWS:, :])
    sums = jax.ShapeDtypeStruct((SUMS, BLK), F32)
    to_core, to_next, base = pl.pallas_call(
        sum_kernel,
        out_shape=(sums, sums, jax.ShapeDtypeStruct((SIDES, filaments), F32)),
        in_specs=[in_vmem] * 3,
        compiler_params=params(),
        cost_estimate=cost(2 * 384 * 96 * 16 * 256, 2000000),
    )(got, resistance[None, :], currents)
    core_pairs = [(g, g ^ 1) for g in range(GROUPS)]
    next_pairs = [(g, (g + (1 if g % 2 else -1)) % GROUPS) for g in range(GROUPS)]
    from_next = lax.ppermute(to_next, "outer", next_pairs)
    from_core = lax.ppermute(to_core, "outer", core_pairs)
    coef = exchange(coef, "outer", OUTER_ORDER)

    return pl.pallas_call(
        final_kernel,
        out_shape=jax.ShapeDtypeStruct((SIDES, filaments), F32),
        compiler_params=params(),
        cost_estimate=cost(2 * SIDES * flat * filaments, 1600000),
    )(coef, col_factors.reshape(flat, filaments), base, from_core, from_next)


def solution(mesh):
    return jax.shard_map(
        on_device,
        mesh=mesh,
        in_specs=(
            P(None, ("outer", "inner")),
            P(("outer", "inner"), None, None, None),
            P(("outer", "inner"), None),
            P(None, None, ("outer", "inner")),
            P(None, None, ("outer", "inner")),
            P(("outer", "inner")),
        ),
        out_specs=P(None, ("outer", "inner")),
        check_vma=False,
    )
```
